32 devices in a mesh: cells: 8 (over y, x, core), bands: 4 (over z).
Axes of the slice: x: 2, y: 2, z: 4, core: 2. Of those that a mesh axis runs over, the one named last changes fastest.
Arguments:
- waves: bfloat16 [256, 16384], P('bands', 'cells'), may hold values from -6 to 6
- stiffness: float32 [125, 125], replicated, as said below
- cell_scale: float32 [1024], P('cells'), may hold values from 0.5 to 4
- potential: float32 [16384], P('cells'), may hold values from -2 to 2
- connect: int32 [125, 1024], P(None, 'cells'), may hold values from 0 to 3071
- live_cells: int32 [8], P('cells'), may hold values from 16 to 128, as said below
- shared: int32 [8, 2, 512], P('cells'), may hold values from 0 to 2047
- window: float32 [2], replicated, may hold values from 1 to 4
Outputs:
- filtered: float32 [256, 16384], P('bands', 'cells')
- projected: float32 [256, 256], P('cells', 'bands')
The draws below stay inside these ranges and needn't reach their ends.
Inputs may be any that keep to these rules, and one draw needn't show every extreme that they name: `live_cells`: at least one partition has all 128 slots live. `stiffness`: symmetric positive definite.
All inputs are finite; a program needn't handle non-finite values.
Results may differ from the reference program's by a relative error of at most 0.0037.
Values may be sent and summed in bfloat16 or wider, within the bound.
A program may use at most 64 MiB of HBM per device.

```python
import math
import jax
import jax.numpy as jnp
from jax import lax

CELL_NODES = 125
WAVES = 256
NODE_DEV = 2048
GHOST = 512
CELL_CAP = 128
CELLS = 1024
NODES = 16384
N_CELLS = 8


def draw_stiffness(key, part):
    normal_draw = jax.random.normal(key, (CELL_NODES, CELL_NODES), jnp.float32)
    return jnp.dot(normal_draw, normal_draw.T) / CELL_NODES + 0.5 * jnp.eye(CELL_NODES, dtype=jnp.float32)


def draw_live_cells(key, part):
    least = max(1, CELL_CAP // 8)
    counts = jax.random.randint(key, (N_CELLS,), least, CELL_CAP // 2 + 1)
    fullest = jax.random.randint(jax.random.fold_in(key, 7), (), 0, N_CELLS)
    return jnp.where(jnp.arange(N_CELLS) == fullest, CELL_CAP, counts).astype(jnp.int32)


def place_ends(values, key, low, high):
    place = [jax.random.randint(jax.random.fold_in(key, axis), (), 0, length) for axis, length in enumerate(values.shape)]
    longest = values.shape.index(max(values.shape))
    neighbour = place[:longest] + [(place[longest] + 1) % values.shape[longest]] + place[longest + 1:]
    return values.at[tuple(place)].set(low).at[tuple(neighbour)].set(high)


def steps_of(key, dims, pieces, low, top_value):
    def one(axis_at, shards_of):
        heights = jax.random.uniform(jax.random.fold_in(jax.random.fold_in(key, 6), axis_at), (shards_of,), jnp.float32, low / len(pieces), top_value / len(pieces))
        return jnp.repeat(jnp.exp(heights), dims[axis_at] // shards_of).reshape((-1,) + (1,) * (len(dims) - axis_at - 1))

    gain = one(*pieces[0])
    for cut in pieces[1:]:
        gain = gain * one(*cut)
    return gain


def gaussian(rng, shape, scale, limit, shards=(), kind=jnp.bfloat16):
    factor_of = steps_of(rng, shape, shards, -0.22, 0.18) if shards else 1.0
    array = jax.random.normal(rng, shape, jnp.float32) * scale * factor_of
    return jnp.minimum(jnp.maximum(array, -limit), limit).astype(kind)


def setup_inputs(seed: int = 0) -> dict:
    splits = jax.random.split(jax.random.key(seed), 9)
    waves = gaussian(splits[0], (WAVES, NODES), 1.0, 6.0, ((0, 4), (1, 8)))
    stiffness = draw_stiffness(jax.random.fold_in(splits[8], 71), 0)
    cell_scale = jnp.clip(jnp.exp(math.log(4.0) - 2.0794415 * jax.random.uniform(splits[2], (CELLS,), jnp.float32) ** steps_of(splits[2], (CELLS,), ((0, 8),), -0.2, 0.2)), 0.5, 4.0)
    potential = jnp.clip(jax.random.uniform(splits[3], (NODES,), jnp.float32, -2.0, 2.0) * steps_of(splits[3], (NODES,), ((0, 8),), -0.4, 0.0), -2.0, 2.0)
    connect = place_ends(jax.random.randint(splits[4], (CELL_NODES, CELLS), 0, NODE_DEV + 2 * GHOST), jax.random.fold_in(splits[4], 1), 0, (NODE_DEV + 2 * GHOST) - 1).astype(jnp.int32)
    live_cells = draw_live_cells(jax.random.fold_in(splits[8], 71), 0)
    shared = place_ends(jax.random.randint(splits[6], (N_CELLS, 2, GHOST), 0, NODE_DEV), jax.random.fold_in(splits[6], 1), 0, NODE_DEV - 1).astype(jnp.int32)
    window = jnp.clip(jax.random.uniform(splits[7], (2,), jnp.float32, 1.0, 4.0), 1.0, 4.0)
    return dict(waves=waves, stiffness=stiffness, cell_scale=cell_scale, potential=potential, connect=connect, live_cells=live_cells, shared=shared, window=window)


sigma_one = -0.5
sigma_two = 1.0 / (2.0 / sigma_one - sigma_one)


def ghost_blocks(blocks, shared):
    picked = jax.vmap(lambda block_rows, rows_list: block_rows[rows_list])(blocks, shared)
    zeros_block = jnp.zeros((1,) + picked.shape[2:], blocks.dtype)
    lower = jnp.concatenate([zeros_block, picked[:-1, 1]], axis=0)
    upper = jnp.concatenate([picked[1:, 0], zeros_block], axis=0)
    return jnp.concatenate([lower, blocks, upper], axis=1)


def cell_terms(extended, connect, scale, live_count, stiff_rounded):
    columns = extended.shape[1]
    gathered = extended[connect].astype(jnp.float32)
    product = jnp.einsum("ij,cjk->cik", stiff_rounded.astype(jnp.float32), gathered)
    weight = scale * (jnp.arange(connect.shape[0]) < live_count).astype(jnp.float32)
    totals = jnp.zeros((extended.shape[0], columns), jnp.float32)
    return totals.at[connect.reshape(-1)].add((product * weight[:, None, None]).reshape(-1, columns))


def apply_operator(blocks, shared, connect, scale, live_cells, stiff_rounded):
    extended = ghost_blocks(blocks, shared)
    totals = lax.map(lambda items: cell_terms(items[0], items[1], items[2], items[3], stiff_rounded),
                     (extended, connect, scale, live_cells))
    own = totals[:, GHOST:GHOST + NODE_DEV]
    zeros_block = jnp.zeros((1, GHOST, totals.shape[2]), jnp.float32)
    from_lower = jnp.concatenate([zeros_block, totals[:-1, GHOST + NODE_DEV:]], axis=0)
    from_upper = jnp.concatenate([totals[1:, :GHOST], zeros_block], axis=0)
    return jax.vmap(lambda owned, rows_list, lower, upper: owned.at[rows_list[0]].add(lower).at[rows_list[1]].add(upper))(
        own, shared, from_lower, from_upper)


def reference(waves, stiffness, cell_scale, potential, connect, live_cells, shared, window):
    stiff_rounded = stiffness.astype(jnp.bfloat16)
    blocks = waves.T.reshape(N_CELLS, NODE_DEV, WAVES)
    node_pot = potential.reshape(N_CELLS, NODE_DEV, 1)
    cell_conn = connect.T.reshape(N_CELLS, CELL_CAP, CELL_NODES)
    scales = cell_scale.reshape(N_CELLS, CELL_CAP)
    center = window[0]
    half_width = window[1]
    waves32 = blocks.astype(jnp.float32)
    applied_x = apply_operator(blocks, shared, cell_conn, scales, live_cells, stiff_rounded) + node_pot * waves32
    first_pass = ((applied_x - center * waves32) * (sigma_one / half_width)).astype(jnp.bfloat16)
    first32 = first_pass.astype(jnp.float32)
    applied_y = apply_operator(first_pass, shared, cell_conn, scales, live_cells, stiff_rounded) + node_pot * first32
    filtered = (applied_y - center * first32) * (2.0 * sigma_two / half_width) - sigma_one * sigma_two * waves32
    wave_rounded = filtered.astype(jnp.bfloat16)
    applied = apply_operator(wave_rounded, shared, cell_conn, scales, live_cells, stiff_rounded) + node_pot * filtered
    apply_rounded = applied.astype(jnp.bfloat16)
    flat_wave = wave_rounded.reshape(NODES, WAVES)
    flat_apply = apply_rounded.reshape(NODES, WAVES)
    projected = jnp.dot(flat_wave.T, flat_apply, preferred_element_type=jnp.float32) / NODES
    return filtered.reshape(NODES, WAVES).T, projected
```

```python
import functools
import math

import jax
import jax.numpy as jnp
from jax import lax
from jax.experimental import pallas as pl
from jax.experimental.pallas import tpu as pltpu
from jax.sharding import PartitionSpec as P

sigma_one = -0.5
sigma_two = 1.0 / (2.0 / sigma_one - sigma_one)

LANES = 128
WAYS = 4


def cell_kernel(
    nodes, capacity, columns, connect, scale, live, stiff, ext, out, x0, x1, p0, p1, *sums
):
    lows, highs = sums[:WAYS], sums[WAYS:]
    rows = ext.shape[0]
    chunk = math.gcd(rows, 256)

    @pl.loop(0, rows // chunk)
    def _(step):
        at = pl.ds(pl.multiple_of(step * chunk, chunk), chunk)
        for total in sums:
            total[at, :] = jnp.zeros((chunk, LANES), jnp.float32)

    low_lanes = lax.broadcasted_iota(jnp.int32, (1, LANES), 1) < columns
    live_count = live[0]
    pairs = (live_count + 1) // 2
    last = capacity // 2 - 1

    def cells_of(pair):
        first = jnp.minimum(pair, last) * 2
        return first, first + 1

    def gather(pair, x):
        first, second = cells_of(pair)
        for j in range(nodes):
            a = connect[j, first]
            b = connect[j, second]
            x[j : j + 1, :] = jnp.where(low_lanes, ext[pl.ds(a, 1), :], ext[pl.ds(b, 1), :])

    def multiply(pair, x, p):
        first, second = cells_of(pair)
        low = jnp.where(pair * 2 < live_count, scale[first], 0.0)
        high = jnp.where(pair * 2 + 1 < live_count, scale[second], 0.0)
        weight = jnp.where(low_lanes, low, high)
        p[...] = weight * jnp.dot(
            stiff[...], x[...].astype(jnp.bfloat16), preferred_element_type=jnp.float32
        )

    def scatter(pair, p):
        first, second = cells_of(pair)
        for begin in range(0, nodes, WAYS):
            todo = []
            for way in range(min(WAYS, nodes - begin)):
                j = begin + way
                term = p[j : j + 1, :]
                for sums_of, cell in ((lows, first), (highs, second)):
                    at = pl.ds(connect[j, cell], 1)
                    todo.append((sums_of[way], at, sums_of[way][at, :] + term))
            for total, at, value in todo:
                total[at, :] = value

    x0[...] = jnp.zeros_like(x0)
    x1[...] = jnp.zeros_like(x1)
    gather(0, x0)
    multiply(0, x0, p0)
    gather(1, x1)

    @pl.loop(0, (pairs + 1) // 2)
    def _(turn):
        pair = turn * 2
        scatter(pair, p0)
        multiply(pair + 1, x1, p1)
        gather(pair + 2, x0)
        scatter(pair + 1, p1)
        multiply(pair + 2, x0, p0)
        gather(pair + 3, x1)

    @pl.loop(0, rows // chunk)
    def _(step):
        at = pl.ds(pl.multiple_of(step * chunk, chunk), chunk)
        low = lows[0][at, :]
        high = highs[0][at, :]
        for way in range(1, WAYS):
            low += lows[way][at, :]
            high += highs[way][at, :]
        out[at, :] = low[:, :columns] + high[:, columns : 2 * columns]


def cell_sums(ext, stiff, connect, scale, live):
    rows, columns = ext.shape
    assert 2 * columns == LANES
    nodes, capacity = connect.shape
    depth = stiff.shape[0]
    vmem = pl.BlockSpec(memory_space=pltpu.VMEM)
    smem = pl.BlockSpec(memory_space=pltpu.SMEM)
    wide = jnp.concatenate([ext, ext], axis=1).astype(jnp.float32)
    return pl.pallas_call(
        functools.partial(cell_kernel, nodes, capacity, columns),
        out_shape=jax.ShapeDtypeStruct((rows, columns), jnp.float32),
        in_specs=[smem, smem, smem, vmem, vmem],
        out_specs=vmem,
        scratch_shapes=[pltpu.VMEM((depth, LANES), jnp.float32)] * 4
        + [pltpu.VMEM((rows, LANES), jnp.float32)] * (2 * WAYS),
        compiler_params=pltpu.CompilerParams(vmem_limit_bytes=40 * 1024 * 1024),
    )(connect, scale, live, stiff, wide)


def local(waves, stiffness, cell_scale, potential, connect, live_cells, shared, window):
    columns, node_dev = waves.shape
    ghost = shared.shape[2]
    low_nodes, high_nodes = shared[0, 0], shared[0, 1]
    nodes = connect.shape[0]
    depth = -(-nodes // LANES) * LANES
    stiff = jnp.pad(stiffness, ((0, depth - nodes), (0, depth - nodes))).astype(jnp.bfloat16)
    center = window[0]
    half_width = window[1]
    potential_col = potential[:, None]
    count = lax.axis_size("cells")
    forward = [(i, i + 1) for i in range(count - 1)]
    backward = [(i + 1, i) for i in range(count - 1)]

    def apply(owned):
        lower = lax.ppermute(owned[high_nodes], "cells", forward)
        upper = lax.ppermute(owned[low_nodes], "cells", backward)
        ext = jnp.concatenate([lower, owned, upper], axis=0)
        totals = cell_sums(ext, stiff, connect, cell_scale, live_cells)
        from_lower = lax.ppermute(totals[ghost + node_dev :], "cells", forward)
        from_upper = lax.ppermute(totals[:ghost], "cells", backward)
        return (
            totals[ghost : ghost + node_dev]
            .at[jnp.concatenate([low_nodes, high_nodes])]
            .add(jnp.concatenate([from_lower, from_upper], axis=0))
        )

    start = waves.T
    start32 = start.astype(jnp.float32)
    applied_x = apply(start) + potential_col * start32
    first_pass = ((applied_x - center * start32) * (sigma_one / half_width)).astype(jnp.bfloat16)
    first32 = first_pass.astype(jnp.float32)
    applied_y = apply(first_pass) + potential_col * first32
    filtered = (applied_y - center * first32) * (
        2.0 * sigma_two / half_width
    ) - sigma_one * sigma_two * start32
    wave_rounded = filtered.astype(jnp.bfloat16)
    gathered = lax.all_gather(wave_rounded, "bands", axis=1, tiled=True)
    applied = apply(wave_rounded) + potential_col * filtered
    apply_rounded = applied.astype(jnp.bfloat16)
    inverse_total = 1.0 / (node_dev * count)
    partial_value = (
        jnp.einsum("nw,nv->wv", gathered, apply_rounded, preferred_element_type=jnp.float32)
        * inverse_total
    )
    projected = lax.psum_scatter(partial_value, "cells", scatter_dimension=0, tiled=True)
    return (filtered.T, projected)


def solution(mesh):
    return jax.shard_map(
        local,
        mesh=mesh,
        in_specs=(
            P("bands", "cells"),
            P(),
            P("cells"),
            P("cells"),
            P(None, "cells"),
            P("cells"),
            P("cells", None, None),
            P(),
        ),
        out_specs=(P("bands", "cells"), P("cells", "bands")),
        check_vma=False,
    )
```

```python
import functools
import math

import jax
import jax.numpy as jnp
from jax import lax
from jax.experimental import pallas as pl
from jax.experimental.pallas import tpu as pltpu
from jax.sharding import PartitionSpec as P

sigma_one = -0.5
sigma_two = 1.0 / (2.0 / sigma_one - sigma_one)

LANES = 128
HALF = LANES // 2
WAYS = 8
SHARED_WAYS = 2
MIB = 1024 * 1024
VMEM = pl.BlockSpec(memory_space=pltpu.VMEM)
SMEM = pl.BlockSpec(memory_space=pltpu.SMEM)


def low_half():
    return lax.broadcasted_iota(jnp.int32, (1, LANES), 1) < HALF


def swapped(block):
    return pltpu.roll(block, HALF, axis=1)


def chunks(rows, body):
    size = math.gcd(rows, 256)

    @pl.loop(0, rows // size)
    def _(step):
        body(pl.ds(pl.multiple_of(step * size, size), size))


def clear(refs):
    def body(at):
        for ref in refs:
            ref[at, :] = jnp.zeros((at.size, LANES), ref.dtype)

    chunks(refs[0].shape[0], body)


def sum_of(refs, at):
    total = refs[0][at, :]
    for ref in refs[1:]:
        total += ref[at, :]
    return total


def cell_kernel(
    nodes,
    capacity,
    connect,
    scale,
    live,
    stiff,
    own,
    from_low,
    from_high,
    out,
    out_low,
    out_high,
    ext,
    x0,
    x1,
    p0,
    p1,
    *sums,
):
    lows, highs = sums[:WAYS], sums[WAYS:]
    node_dev = own.shape[0]
    half = from_low.shape[0]
    low_lanes = low_half()
    clear(sums)

    def copy_own(at):
        ext[pl.ds(pl.multiple_of(at.start + 2 * half, at.size), at.size), :] = own[at, :]

    chunks(node_dev, copy_own)
    for first_row, part in ((0, from_low), (2 * half + node_dev, from_high)):
        value = part[...].astype(jnp.float32)
        other = swapped(value)
        ext[first_row : first_row + half, :] = jnp.where(low_lanes, value, other)
        ext[first_row + half : first_row + 2 * half, :] = jnp.where(low_lanes, other, value)

    live_count = live[0]
    pairs = (live_count + 1) // 2
    last = capacity // 2 - 1

    def cells_of(pair):
        first = jnp.minimum(pair, last) * 2
        return first, first + 1

    def move(scatter_pair, p, gather_pair, x):
        for begin in range(0, nodes, WAYS):
            todo = []
            for way in range(min(WAYS, nodes - begin)):
                j = begin + way
                if p is not None:
                    term = p[j : j + 1, :]
                    for sums_of, cell in zip((lows, highs), cells_of(scatter_pair)):
                        at = pl.ds(connect[j, cell], 1)
                        todo.append((sums_of[way], at, sums_of[way][at, :] + term))
                first, second = cells_of(gather_pair)
                low = ext[pl.ds(connect[j, first], 1), :]
                high = ext[pl.ds(connect[j, second], 1), :]
                todo.append((x, pl.ds(j, 1), jnp.where(low_lanes, low, high)))
            for ref, at, value in todo:
                ref[at, :] = value

    def multiply(pair, x, p):
        first, second = cells_of(pair)
        low = jnp.where(pair * 2 < live_count, scale[first], 0.0)
        high = jnp.where(pair * 2 + 1 < live_count, scale[second], 0.0)
        weight = jnp.where(low_lanes, low, high)
        p[...] = weight * jnp.dot(
            stiff[...], x[...].astype(jnp.bfloat16), preferred_element_type=jnp.float32
        )

    x0[...] = jnp.zeros_like(x0)
    x1[...] = jnp.zeros_like(x1)
    move(0, None, 0, x0)
    multiply(0, x0, p0)
    move(0, None, 1, x1)

    @pl.loop(0, (pairs + 1) // 2)
    def _(turn):
        pair = turn * 2
        multiply(pair + 1, x1, p1)
        move(pair, p0, pair + 2, x0)
        multiply(pair + 2, x0, p0)
        move(pair + 1, p1, pair + 3, x1)

    def total(at):
        both = jnp.where(low_lanes, sum_of(lows, at), sum_of(highs, at))
        return both + swapped(both)

    def write_own(at):
        out[at, :] = total(pl.ds(pl.multiple_of(at.start + 2 * half, at.size), at.size))

    chunks(node_dev, write_own)
    for first_row, part in ((0, out_low), (2 * half + node_dev, out_high)):
        part[...] = jnp.where(
            low_lanes, total(pl.ds(first_row, half)), total(pl.ds(first_row + half, half))
        )


def cell_sums(own, from_low, from_high, stiff, connect, scale, live):
    nodes, capacity = connect.shape
    depth = stiff.shape[0]
    half = from_low.shape[0]
    rows = own.shape[0] + 4 * half
    return pl.pallas_call(
        functools.partial(cell_kernel, nodes, capacity),
        out_shape=[jax.ShapeDtypeStruct(own.shape, jnp.float32)]
        + [jax.ShapeDtypeStruct((half, LANES), jnp.float32)] * 2,
        in_specs=[SMEM, SMEM, SMEM] + [VMEM] * 4,
        out_specs=[VMEM] * 3,
        scratch_shapes=[pltpu.VMEM((rows, LANES), jnp.float32)]
        + [pltpu.VMEM((depth, LANES), jnp.float32)] * 4
        + [pltpu.VMEM((rows, LANES), jnp.float32)] * (2 * WAYS),
        compiler_params=pltpu.CompilerParams(vmem_limit_bytes=48 * MIB),
    )(connect, scale, live, stiff, own, from_low, from_high)


def gather_shared(shared, half, wide, send_low, send_high):
    low_lanes = low_half()
    group = math.gcd(half, 16)

    @pl.loop(0, half // group)
    def _(turn):
        todo = []
        for k in range(group):
            j = turn * group + k
            for side, send in ((0, send_low), (1, send_high)):
                first = wide[pl.ds(shared[side, j], 1), :]
                second = wide[pl.ds(shared[side, j + half], 1), :]
                todo.append((send, pl.ds(j, 1), jnp.where(low_lanes, first, second)))
        for ref, at, value in todo:
            ref[at, :] = value


def gather_kernel(shared, wide, send_low, send_high, packed_low, packed_high):
    half = packed_low.shape[0]
    gather_shared(shared, half, wide, packed_low, packed_high)
    send_low[...] = packed_low[...].astype(send_low.dtype)
    send_high[...] = packed_high[...].astype(send_high.dtype)


def first_sends(shared, wide):
    half = shared.shape[1] // 2
    return pl.pallas_call(
        gather_kernel,
        out_shape=[jax.ShapeDtypeStruct((half, LANES), jnp.bfloat16)] * 2,
        in_specs=[SMEM, VMEM],
        out_specs=[VMEM] * 2,
        scratch_shapes=[pltpu.VMEM((half, LANES), jnp.float32)] * 2,
    )(shared, wide)


def assemble_kernel(stage, shared, window, totals, from_low, from_high, potential, before, start, *refs):
    outs = {"first": 3, "second": 4, "third": 1}[stage]
    out, scratch = refs[:outs], refs[outs:]
    sums, scratch = scratch[: 4 * SHARED_WAYS], scratch[4 * SHARED_WAYS :]
    half = from_low.shape[0]
    low_lanes = low_half()
    clear(sums)
    group = math.gcd(half, 8)

    @pl.loop(0, half // group)
    def _(turn):
        for begin in range(0, group, SHARED_WAYS):
            todo = []
            for way in range(SHARED_WAYS):
                j = turn * group + begin + way
                for side, part in ((0, from_low), (1, from_high)):
                    term = part[pl.ds(j, 1), :]
                    for upper in range(2):
                        total = sums[way * 4 + side * 2 + upper]
                        at = pl.ds(shared[side, j + upper * half], 1)
                        todo.append((total, at, total[at, :] + term))
            for ref, at, value in todo:
                ref[at, :] = value

    center = window[0]
    half_width = window[1]
    lows = [sums[k] for k in range(0, len(sums), 2)]
    highs = [sums[k] for k in range(1, len(sums), 2)]

    def pointwise(at):
        both = jnp.where(low_lanes, sum_of(lows, at), sum_of(highs, at))
        value = before[at, :]
        applied = totals[at, :] + (both + swapped(both)) + potential[at, :] * value
        if stage == "first":
            passed = (applied - center * value) * (sigma_one / half_width)
            out[0][at, :] = passed.astype(jnp.bfloat16).astype(jnp.float32)
        elif stage == "second":
            filtered = (applied - center * value) * (
                2.0 * sigma_two / half_width
            ) - sigma_one * sigma_two * start[at, :]
            out[3][at, :] = filtered
            out[0][at, :] = filtered.astype(jnp.bfloat16).astype(jnp.float32)
        else:
            out[0][at, :] = applied

    chunks(totals.shape[0], pointwise)
    if stage != "third":
        gather_shared(shared, half, out[0], scratch[0], scratch[1])
        out[1][...] = scratch[0][...].astype(out[1].dtype)
        out[2][...] = scratch[1][...].astype(out[2].dtype)


def assemble(stage, shared, window, totals, from_low, from_high, potential, before, start):
    half = from_low.shape[0]
    whole = jax.ShapeDtypeStruct(totals.shape, jnp.float32)
    packed = jax.ShapeDtypeStruct((half, LANES), jnp.bfloat16)
    out_shape = {
        "first": [whole, packed, packed],
        "second": [whole, packed, packed, whole],
        "third": [whole],
    }[stage]
    return pl.pallas_call(
        functools.partial(assemble_kernel, stage),
        out_shape=out_shape,
        in_specs=[SMEM, SMEM] + [VMEM] * 6,
        out_specs=[VMEM] * len(out_shape),
        scratch_shapes=[pltpu.VMEM(totals.shape, jnp.float32)] * (4 * SHARED_WAYS)
        + [pltpu.VMEM((half, LANES), jnp.float32)] * 2,
        compiler_params=pltpu.CompilerParams(vmem_limit_bytes=32 * MIB),
    )(shared, window, totals, from_low, from_high, potential, before, start)


def exchange_kernel(count, send_low, send_high, from_low, from_high, slot_low, slot_high, sems):
    me = lax.axis_index("cells")
    has_low = me > 0
    has_high = me < count - 1
    barrier = pltpu.get_barrier_semaphore()

    @pl.when(has_low)
    def _():
        pl.semaphore_signal(
            barrier, inc=1, device_id={"cells": me - 1}, device_id_type=pl.DeviceIdType.MESH
        )

    @pl.when(has_high)
    def _():
        pl.semaphore_signal(
            barrier, inc=1, device_id={"cells": me + 1}, device_id_type=pl.DeviceIdType.MESH
        )

    pl.semaphore_wait(barrier, jnp.minimum(me, 1) + jnp.minimum(count - 1 - me, 1))

    def copy(source, slot, place, target):
        return pltpu.make_async_remote_copy(
            src_ref=source,
            dst_ref=slot,
            send_sem=sems.at[place],
            recv_sem=sems.at[place + 1],
            device_id={"cells": target},
            device_id_type=pl.DeviceIdType.MESH,
        )

    down = copy(send_low, slot_high, 0, me - 1)
    up = copy(send_high, slot_low, 2, me + 1)

    @pl.when(has_low)
    def _():
        down.start()

    @pl.when(has_high)
    def _():
        up.start()

    @pl.when(has_low)
    def _():
        up.wait_recv()
        from_low[...] = slot_low[...]

    @pl.when(jnp.logical_not(has_low))
    def _():
        from_low[...] = jnp.zeros_like(from_low)

    @pl.when(has_high)
    def _():
        down.wait_recv()
        from_high[...] = slot_high[...]

    @pl.when(jnp.logical_not(has_high))
    def _():
        from_high[...] = jnp.zeros_like(from_high)

    @pl.when(has_low)
    def _():
        down.wait_send()

    @pl.when(has_high)
    def _():
        up.wait_send()


def exchange(send_low, send_high, collective_id):
    shape = jax.ShapeDtypeStruct(send_low.shape, send_low.dtype)
    return pl.pallas_call(
        functools.partial(exchange_kernel, lax.axis_size("cells")),
        out_shape=[shape] * 2,
        in_specs=[VMEM] * 2,
        out_specs=[VMEM] * 2,
        scratch_shapes=[pltpu.VMEM(send_low.shape, send_low.dtype)] * 2
        + [pltpu.SemaphoreType.DMA((4,))],
        compiler_params=pltpu.CompilerParams(collective_id=collective_id, has_side_effects=True),
    )(send_low, send_high)


def reduce_kernel(count, parts, out, slots, send_sems, recv_sems):
    me = lax.axis_index("cells")
    barrier = pltpu.get_barrier_semaphore()

    @pl.loop(1, count)
    def _(step):
        pl.semaphore_signal(
            barrier,
            inc=1,
            device_id={"cells": lax.rem(me + step, count)},
            device_id_type=pl.DeviceIdType.MESH,
        )

    pl.semaphore_wait(barrier, count - 1)

    def copy(step):
        target = lax.rem(me + step, count)
        return pltpu.make_async_remote_copy(
            src_ref=parts.at[target],
            dst_ref=slots.at[step],
            send_sem=send_sems.at[step],
            recv_sem=recv_sems.at[step],
            device_id={"cells": target},
            device_id_type=pl.DeviceIdType.MESH,
        )

    @pl.loop(1, count)
    def _(step):
        copy(step).start()

    out[...] = parts[me]

    @pl.loop(1, count)
    def _(step):
        copy(step).wait_recv()
        out[...] += slots[step]

    @pl.loop(1, count)
    def _(step):
        copy(step).wait_send()


def reduce_parts(parts, collective_id):
    count, rows, columns = parts.shape
    return pl.pallas_call(
        functools.partial(reduce_kernel, count),
        out_shape=jax.ShapeDtypeStruct((rows, columns), jnp.float32),
        in_specs=[VMEM],
        out_specs=VMEM,
        scratch_shapes=[
            pltpu.VMEM(parts.shape, jnp.float32),
            pltpu.SemaphoreType.DMA((count,)),
            pltpu.SemaphoreType.DMA((count,)),
        ],
        compiler_params=pltpu.CompilerParams(collective_id=collective_id, has_side_effects=True),
    )(parts)


def local(waves, stiffness, cell_scale, potential, connect, live_cells, shared, window):
    columns, node_dev = waves.shape
    assert columns == HALF
    nodes = connect.shape[0]
    depth = -(-nodes // LANES) * LANES
    stiff = jnp.pad(stiffness, ((0, depth - nodes), (0, depth - nodes))).astype(jnp.bfloat16)
    lists = shared[0]
    potential_wide = jnp.broadcast_to(potential[:, None], (node_dev, LANES))
    count = lax.axis_size("cells")

    def totals_of(own, send_low, send_high):
        from_low, from_high = exchange(send_low, send_high, 0)
        totals, to_low, to_high = cell_sums(
            own, from_low, from_high, stiff, connect, cell_scale, live_cells
        )
        return totals, *exchange(to_low, to_high, 1)

    start = jnp.concatenate([waves, waves], axis=0).T.astype(jnp.float32)
    first, *sends = assemble(
        "first",
        lists,
        window,
        *totals_of(start, *first_sends(lists, start)),
        potential_wide,
        start,
        start,
    )
    second, send_low, send_high, filtered = assemble(
        "second", lists, window, *totals_of(first, *sends), potential_wide, first, start
    )
    wave_rounded = second[:, :columns].astype(jnp.bfloat16)
    gathered = lax.all_gather(wave_rounded, "bands", axis=1, tiled=True)
    (applied,) = assemble(
        "third",
        lists,
        window,
        *totals_of(second, send_low, send_high),
        potential_wide,
        filtered,
        start,
    )
    apply_rounded = applied[:, :columns].astype(jnp.bfloat16)
    partial_value = jnp.einsum(
        "nw,nv->wv", gathered, apply_rounded, preferred_element_type=jnp.float32
    ) * (1.0 / (node_dev * count))
    projected = reduce_parts(partial_value.reshape(count, -1, columns), 2)
    return (filtered[:, :columns].T, projected)


def solution(mesh):
    return jax.shard_map(
        local,
        mesh=mesh,
        in_specs=(
            P("bands", "cells"),
            P(),
            P("cells"),
            P("cells"),
            P(None, "cells"),
            P("cells"),
            P("cells", None, None),
            P(),
        ),
        out_specs=(P("bands", "cells"), P("cells", "bands")),
        check_vma=False,
    )
```

```python
import functools
import math

import jax
import jax.numpy as jnp
from jax import lax
from jax.experimental import pallas as pl
from jax.experimental.pallas import tpu as pltpu
from jax.sharding import PartitionSpec as P

sigma_one = -0.5
sigma_two = 1.0 / (2.0 / sigma_one - sigma_one)

LANES = 128
HALF = LANES // 2
WAYS = 4
SHARED_WAYS = 2
MIB = 1024 * 1024
VMEM = pl.BlockSpec(memory_space=pltpu.VMEM)
SMEM = pl.BlockSpec(memory_space=pltpu.SMEM)


def low_half():
    return lax.broadcasted_iota(jnp.int32, (1, LANES), 1) < HALF


def swapped(block):
    return pltpu.roll(block, HALF, axis=1)


def chunks(rows, body):
    size = math.gcd(rows, 256)

    @pl.loop(0, rows // size)
    def _(step):
        body(pl.ds(pl.multiple_of(step * size, size), size))


def clear(refs):
    def body(at):
        for ref in refs:
            ref[at, :] = jnp.zeros((at.size, LANES), ref.dtype)

    chunks(refs[0].shape[0], body)


def sum_of(refs, at):
    total = refs[0][at, :]
    for ref in refs[1:]:
        total += ref[at, :]
    return total


def cell_kernel(
    nodes,
    capacity,
    connect,
    scale,
    live,
    stiff,
    ext,
    out,
    out_low,
    out_high,
    x0,
    x1,
    p0,
    p1,
    *sums,
):
    lows, highs = sums[:WAYS], sums[WAYS:]
    node_dev = out.shape[0]
    half = out_low.shape[0]
    low_lanes = low_half()
    clear(sums)

    live_count = live[0]
    pairs = (live_count + 1) // 2
    last = capacity // 2 - 1

    def cells_of(pair):
        first = jnp.minimum(pair, last) * 2
        return first, first + 1

    def move(scatter_pair, p, gather_pair, x):
        for begin in range(0, nodes, WAYS):
            todo = []
            for way in range(min(WAYS, nodes - begin)):
                j = begin + way
                if p is not None:
                    term = p[j : j + 1, :]
                    for sums_of, cell in zip((lows, highs), cells_of(scatter_pair)):
                        at = pl.ds(connect[j, cell], 1)
                        todo.append((sums_of[way], at, sums_of[way][at, :] + term))
                first, second = cells_of(gather_pair)
                low = ext[connect[j, first]]
                high = ext[connect[j, second]]
                todo.append((x, pl.ds(j, 1), jnp.where(low_lanes, low, high)))
            for ref, at, value in todo:
                ref[at, :] = value

    def multiply(pair, x, p):
        first, second = cells_of(pair)
        low = jnp.where(pair * 2 < live_count, scale[first], 0.0)
        high = jnp.where(pair * 2 + 1 < live_count, scale[second], 0.0)
        weight = jnp.where(low_lanes, low, high)
        p[...] = weight * jnp.dot(
            stiff[...], x[...].astype(jnp.bfloat16), preferred_element_type=jnp.float32
        )

    x0[...] = jnp.zeros_like(x0)
    x1[...] = jnp.zeros_like(x1)
    move(0, None, 0, x0)
    multiply(0, x0, p0)
    move(0, None, 1, x1)

    @pl.loop(0, (pairs + 1) // 2)
    def _(turn):
        pair = turn * 2
        multiply(pair + 1, x1, p1)
        move(pair, p0, pair + 2, x0)
        multiply(pair + 2, x0, p0)
        move(pair + 1, p1, pair + 3, x1)

    def total(at):
        both = jnp.where(low_lanes, sum_of(lows, at), sum_of(highs, at))
        return both + swapped(both)

    def write_own(at):
        out[at, :] = total(pl.ds(pl.multiple_of(at.start + 2 * half, at.size), at.size))

    chunks(node_dev, write_own)
    for first_row, part in ((0, out_low), (2 * half + node_dev, out_high)):
        part[...] = jnp.where(
            low_lanes, total(pl.ds(first_row, half)), total(pl.ds(first_row + half, half))
        )


def cell_sums(ext, node_dev, stiff, connect, scale, live):
    nodes, capacity = connect.shape
    depth = stiff.shape[0]
    rows = ext.shape[0]
    half = (rows - node_dev) // 4
    return pl.pallas_call(
        functools.partial(cell_kernel, nodes, capacity),
        out_shape=[jax.ShapeDtypeStruct((node_dev, LANES), jnp.float32)]
        + [jax.ShapeDtypeStruct((half, LANES), jnp.float32)] * 2,
        in_specs=[SMEM, SMEM, SMEM] + [VMEM] * 2,
        out_specs=[VMEM] * 3,
        scratch_shapes=[pltpu.VMEM((depth, LANES), jnp.float32)] * 4
        + [pltpu.VMEM((rows, LANES), jnp.float32)] * (2 * WAYS),
        compiler_params=pltpu.CompilerParams(vmem_limit_bytes=24 * MIB),
    )(connect, scale, live, stiff, ext.reshape(rows, 1, LANES))


def gather_shared(shared, half, wide, send_low, send_high):
    low_lanes = low_half()
    group = math.gcd(half, 16)

    @pl.loop(0, half // group)
    def _(turn):
        todo = []
        for k in range(group):
            j = turn * group + k
            for side, send in ((0, send_low), (1, send_high)):
                first = wide[pl.ds(shared[side, j], 1), :]
                second = wide[pl.ds(shared[side, j + half], 1), :]
                todo.append((send, pl.ds(j, 1), jnp.where(low_lanes, first, second)))
        for ref, at, value in todo:
            ref[at, :] = value


def gather_kernel(shared, wide, send_low, send_high, packed_low, packed_high):
    half = packed_low.shape[0]
    gather_shared(shared, half, wide, packed_low, packed_high)
    send_low[...] = packed_low[...].astype(send_low.dtype)
    send_high[...] = packed_high[...].astype(send_high.dtype)


def first_sends(shared, wide):
    half = shared.shape[1] // 2
    return pl.pallas_call(
        gather_kernel,
        out_shape=[jax.ShapeDtypeStruct((half, LANES), jnp.bfloat16)] * 2,
        in_specs=[SMEM, VMEM],
        out_specs=[VMEM] * 2,
        scratch_shapes=[pltpu.VMEM((half, LANES), jnp.float32)] * 2,
        compiler_params=pltpu.CompilerParams(vmem_limit_bytes=8 * MIB),
    )(shared, wide)


def assemble_kernel(stage, shared, window, totals, from_low, from_high, potential, before, start, *refs):
    outs = {"first": 3, "second": 4, "third": 1}[stage]
    out, scratch = refs[:outs], refs[outs:]
    sums, scratch = scratch[: 4 * SHARED_WAYS], scratch[4 * SHARED_WAYS :]
    half = from_low.shape[0]
    low_lanes = low_half()
    clear(sums)
    group = math.gcd(half, 8)

    @pl.loop(0, half // group)
    def _(turn):
        for begin in range(0, group, SHARED_WAYS):
            todo = []
            for way in range(SHARED_WAYS):
                j = turn * group + begin + way
                for side, part in ((0, from_low), (1, from_high)):
                    term = part[pl.ds(j, 1), :]
                    for upper in range(2):
                        total = sums[way * 4 + side * 2 + upper]
                        at = pl.ds(shared[side, j + upper * half], 1)
                        todo.append((total, at, total[at, :] + term))
            for ref, at, value in todo:
                ref[at, :] = value

    center = window[0]
    half_width = window[1]
    lows = [sums[k] for k in range(0, len(sums), 2)]
    highs = [sums[k] for k in range(1, len(sums), 2)]

    def pointwise(at):
        both = jnp.where(low_lanes, sum_of(lows, at), sum_of(highs, at))
        value = before[at, :]
        applied = totals[at, :] + (both + swapped(both)) + potential[at, :] * value
        if stage == "first":
            passed = (applied - center * value) * (sigma_one / half_width)
            out[0][at, :] = passed.astype(jnp.bfloat16).astype(jnp.float32)
        elif stage == "second":
            filtered = (applied - center * value) * (
                2.0 * sigma_two / half_width
            ) - sigma_one * sigma_two * start[at, :]
            out[3][at, :] = filtered
            out[0][at, :] = filtered.astype(jnp.bfloat16).astype(jnp.float32)
        else:
            out[0][at, :] = applied

    chunks(totals.shape[0], pointwise)
    if stage != "third":
        gather_shared(shared, half, out[0], scratch[0], scratch[1])
        out[1][...] = scratch[0][...].astype(out[1].dtype)
        out[2][...] = scratch[1][...].astype(out[2].dtype)


def assemble(stage, shared, window, totals, from_low, from_high, potential, before, start):
    half = from_low.shape[0]
    whole = jax.ShapeDtypeStruct(totals.shape, jnp.float32)
    packed = jax.ShapeDtypeStruct((half, LANES), jnp.bfloat16)
    out_shape = {
        "first": [whole, packed, packed],
        "second": [whole, packed, packed, whole],
        "third": [whole],
    }[stage]
    return pl.pallas_call(
        functools.partial(assemble_kernel, stage),
        out_shape=out_shape,
        in_specs=[SMEM, SMEM] + [VMEM] * 6,
        out_specs=[VMEM] * len(out_shape),
        scratch_shapes=[pltpu.VMEM(totals.shape, jnp.float32)] * (4 * SHARED_WAYS)
        + [pltpu.VMEM((half, LANES), jnp.float32)] * 2,
        compiler_params=pltpu.CompilerParams(vmem_limit_bytes=20 * MIB),
    )(shared, window, totals, from_low, from_high, potential, before, start)


def exchange(count, send_low, send_high, slot_low, slot_high, sems, meanwhile):
    me = lax.axis_index("cells")
    has_low = me > 0
    has_high = me < count - 1
    barrier = pltpu.get_barrier_semaphore()

    @pl.when(has_low)
    def _():
        pl.semaphore_signal(
            barrier, inc=1, device_id={"cells": me - 1}, device_id_type=pl.DeviceIdType.MESH
        )

    @pl.when(has_high)
    def _():
        pl.semaphore_signal(
            barrier, inc=1, device_id={"cells": me + 1}, device_id_type=pl.DeviceIdType.MESH
        )

    pl.semaphore_wait(barrier, jnp.minimum(me, 1) + jnp.minimum(count - 1 - me, 1))

    def copy(source, slot, place, target):
        return pltpu.make_async_remote_copy(
            src_ref=source,
            dst_ref=slot,
            send_sem=sems.at[place],
            recv_sem=sems.at[place + 1],
            device_id={"cells": target},
            device_id_type=pl.DeviceIdType.MESH,
        )

    down = copy(send_low, slot_high, 0, me - 1)
    up = copy(send_high, slot_low, 2, me + 1)

    @pl.when(has_low)
    def _():
        down.start()

    @pl.when(has_high)
    def _():
        up.start()

    meanwhile()

    @pl.when(has_low)
    def _():
        up.wait_recv()

    @pl.when(jnp.logical_not(has_low))
    def _():
        slot_low[...] = jnp.zeros_like(slot_low)

    @pl.when(has_high)
    def _():
        down.wait_recv()

    @pl.when(jnp.logical_not(has_high))
    def _():
        slot_high[...] = jnp.zeros_like(slot_high)

    @pl.when(has_low)
    def _():
        down.wait_send()

    @pl.when(has_high)
    def _():
        up.wait_send()


def extend_kernel(count, own, send_low, send_high, ext, slot_low, slot_high, sems):
    node_dev = own.shape[0]
    half = send_low.shape[0]
    low_lanes = low_half()

    def copy_own(at):
        ext[pl.ds(pl.multiple_of(at.start + 2 * half, at.size), at.size), :] = own[at, :]

    exchange(
        count,
        send_low,
        send_high,
        slot_low,
        slot_high,
        sems,
        lambda: chunks(node_dev, copy_own),
    )
    for first_row, part in ((0, slot_low), (2 * half + node_dev, slot_high)):
        value = part[...].astype(jnp.float32)
        other = swapped(value)
        ext[first_row : first_row + half, :] = jnp.where(low_lanes, value, other)
        ext[first_row + half : first_row + 2 * half, :] = jnp.where(low_lanes, other, value)


def swap_kernel(count, send_low, send_high, from_low, from_high, slot_low, slot_high, sems):
    exchange(count, send_low, send_high, slot_low, slot_high, sems, lambda: None)
    from_low[...] = slot_low[...]
    from_high[...] = slot_high[...]


def exchange_call(kernel, collective_id, out_shape, like, *operands):
    return pl.pallas_call(
        functools.partial(kernel, lax.axis_size("cells")),
        out_shape=out_shape,
        in_specs=[VMEM] * len(operands),
        out_specs=[VMEM] * len(out_shape),
        scratch_shapes=[pltpu.VMEM(like.shape, like.dtype)] * 2
        + [pltpu.SemaphoreType.DMA((4,))],
        compiler_params=pltpu.CompilerParams(
            collective_id=collective_id, has_side_effects=True, vmem_limit_bytes=8 * MIB
        ),
    )(*operands)


def extend(own, send_low, send_high):
    rows = own.shape[0] + 4 * send_low.shape[0]
    shape = jax.ShapeDtypeStruct((rows, LANES), jnp.float32)
    return exchange_call(extend_kernel, 0, [shape], send_low, own, send_low, send_high)[0]


def swap(send_low, send_high):
    shape = jax.ShapeDtypeStruct(send_low.shape, send_low.dtype)
    return exchange_call(swap_kernel, 1, [shape] * 2, send_low, send_low, send_high)


def reduce_kernel(count, parts, out, slots, send_sems, recv_sems):
    me = lax.axis_index("cells")
    barrier = pltpu.get_barrier_semaphore()

    @pl.loop(1, count)
    def _(step):
        pl.semaphore_signal(
            barrier,
            inc=1,
            device_id={"cells": lax.rem(me + step, count)},
            device_id_type=pl.DeviceIdType.MESH,
        )

    pl.semaphore_wait(barrier, count - 1)

    def copy(step):
        target = lax.rem(me + step, count)
        return pltpu.make_async_remote_copy(
            src_ref=parts.at[target],
            dst_ref=slots.at[step],
            send_sem=send_sems.at[step],
            recv_sem=recv_sems.at[step],
            device_id={"cells": target},
            device_id_type=pl.DeviceIdType.MESH,
        )

    @pl.loop(1, count)
    def _(step):
        copy(step).start()

    out[...] = parts[me]

    @pl.loop(1, count)
    def _(step):
        copy(step).wait_recv()
        out[...] += slots[step]

    @pl.loop(1, count)
    def _(step):
        copy(step).wait_send()


def reduce_parts(parts, collective_id):
    count, rows, columns = parts.shape
    return pl.pallas_call(
        functools.partial(reduce_kernel, count),
        out_shape=jax.ShapeDtypeStruct((rows, columns), jnp.float32),
        in_specs=[VMEM],
        out_specs=VMEM,
        scratch_shapes=[
            pltpu.VMEM(parts.shape, jnp.float32),
            pltpu.SemaphoreType.DMA((count,)),
            pltpu.SemaphoreType.DMA((count,)),
        ],
        compiler_params=pltpu.CompilerParams(
            collective_id=collective_id, has_side_effects=True, vmem_limit_bytes=8 * MIB
        ),
    )(parts)


def local(waves, stiffness, cell_scale, potential, connect, live_cells, shared, window):
    columns, node_dev = waves.shape
    assert columns == HALF
    nodes = connect.shape[0]
    depth = -(-nodes // LANES) * LANES
    stiff = jnp.pad(stiffness, ((0, depth - nodes), (0, depth - nodes))).astype(jnp.bfloat16)
    lists = shared[0]
    potential_wide = jnp.broadcast_to(potential[:, None], (node_dev, LANES))
    count = lax.axis_size("cells")

    def totals_of(own, send_low, send_high):
        totals, to_low, to_high = cell_sums(
            extend(own, send_low, send_high), node_dev, stiff, connect, cell_scale, live_cells
        )
        return totals, *swap(to_low, to_high)

    start = jnp.concatenate([waves, waves], axis=0).T.astype(jnp.float32)
    first, *sends = assemble(
        "first",
        lists,
        window,
        *totals_of(start, *first_sends(lists, start)),
        potential_wide,
        start,
        start,
    )
    second, send_low, send_high, filtered = assemble(
        "second", lists, window, *totals_of(first, *sends), potential_wide, first, start
    )
    wave_rounded = second[:, :columns].astype(jnp.bfloat16)
    gathered = lax.all_gather(wave_rounded, "bands", axis=1, tiled=True)
    (applied,) = assemble(
        "third",
        lists,
        window,
        *totals_of(second, send_low, send_high),
        potential_wide,
        filtered,
        start,
    )
    apply_rounded = applied[:, :columns].astype(jnp.bfloat16)
    partial_value = jnp.einsum(
        "nw,nv->wv", gathered, apply_rounded, preferred_element_type=jnp.float32
    ) * (1.0 / (node_dev * count))
    projected = reduce_parts(partial_value.reshape(count, -1, columns), 2)
    return (filtered[:, :columns].T, projected)


def solution(mesh):
    return jax.shard_map(
        local,
        mesh=mesh,
        in_specs=(
            P("bands", "cells"),
            P(),
            P("cells"),
            P("cells"),
            P(None, "cells"),
            P("cells"),
            P("cells", None, None),
            P(),
        ),
        out_specs=(P("bands", "cells"), P("cells", "bands")),
        check_vma=False,
    )
```

```python
import functools
import math

import jax
import jax.numpy as jnp
from jax import lax
from jax.experimental import pallas as pl
from jax.experimental.pallas import tpu as pltpu
from jax.sharding import PartitionSpec as P

sigma_one = -0.5
sigma_two = 1.0 / (2.0 / sigma_one - sigma_one)

LANES = 128
HALF = LANES // 2
WAYS = 4
PAIRS = 2
SHARED_WAYS = 2
MIB = 1024 * 1024
VMEM = pl.BlockSpec(memory_space=pltpu.VMEM)
SMEM = pl.BlockSpec(memory_space=pltpu.SMEM)


def low_half():
    return lax.broadcasted_iota(jnp.int32, (1, LANES), 1) < HALF


def swapped(block):
    return pltpu.roll(block, HALF, axis=1)


def chunks(rows, body):
    size = math.gcd(rows, 256)

    @pl.loop(0, rows // size)
    def _(step):
        body(pl.ds(pl.multiple_of(step * size, size), size))


def clear(refs):
    def body(at):
        for ref in refs:
            ref[at, :] = jnp.zeros((at.size, LANES), ref.dtype)

    chunks(refs[0].shape[0], body)


def sum_of(refs, at):
    total = refs[0][at, :]
    for ref in refs[1:]:
        total += ref[at, :]
    return total


def cell_kernel(
    nodes,
    capacity,
    connect,
    scale,
    live,
    stiff,
    ext,
    out,
    out_low,
    out_high,
    x0,
    x1,
    p0,
    p1,
    *sums,
):
    lows, highs = sums[:WAYS], sums[WAYS:]
    node_dev = out.shape[0]
    half = out_low.shape[0]
    low_lanes = low_half()
    clear(sums)

    live_count = live[0]
    batch = 2 * PAIRS
    steps = (live_count + batch - 1) // batch
    last = capacity // batch - 1
    turn_rows = WAYS // PAIRS
    lanes = [slice(k * LANES, (k + 1) * LANES) for k in range(PAIRS)]

    def first_cell(step):
        return jnp.minimum(step, last) * batch

    def move(scatter_step, p, gather_step, x):
        done = first_cell(scatter_step)
        begun = first_cell(gather_step)
        for begin in range(0, nodes, turn_rows):
            todo = []
            for row in range(min(turn_rows, nodes - begin)):
                j = begin + row
                for k in range(PAIRS):
                    if p is not None:
                        term = p[j : j + 1, lanes[k]]
                        for side, sums_of in enumerate((lows, highs)):
                            total = sums_of[row * PAIRS + k]
                            at = pl.ds(connect[j, done + 2 * k + side], 1)
                            todo.append((total, (at, slice(None)), total[at, :] + term))
                    low = ext[connect[j, begun + 2 * k]]
                    high = ext[connect[j, begun + 2 * k + 1]]
                    todo.append((x, (pl.ds(j, 1), lanes[k]), jnp.where(low_lanes, low, high)))
            for ref, at, value in todo:
                ref[at] = value

    def multiply(step, x, p):
        cell = first_cell(step)
        weights = [
            jnp.where(step * batch + k < live_count, scale[cell + k], 0.0) for k in range(batch)
        ]
        product = jnp.dot(
            stiff[...], x[...].astype(jnp.bfloat16), preferred_element_type=jnp.float32
        )
        for k in range(PAIRS):
            weight = jnp.where(low_lanes, weights[2 * k], weights[2 * k + 1])
            p[:, lanes[k]] = weight * product[:, lanes[k]]

    x0[...] = jnp.zeros_like(x0)
    x1[...] = jnp.zeros_like(x1)
    move(0, None, 0, x0)
    multiply(0, x0, p0)
    move(0, None, 1, x1)

    @pl.loop(0, (steps + 1) // 2)
    def _(turn):
        step = turn * 2
        multiply(step + 1, x1, p1)
        move(step, p0, step + 2, x0)
        multiply(step + 2, x0, p0)
        move(step + 1, p1, step + 3, x1)

    def total(at):
        both = jnp.where(low_lanes, sum_of(lows, at), sum_of(highs, at))
        return both + swapped(both)

    def write_own(at):
        out[at, :] = total(pl.ds(pl.multiple_of(at.start + 2 * half, at.size), at.size))

    chunks(node_dev, write_own)
    for first_row, part in ((0, out_low), (2 * half + node_dev, out_high)):
        part[...] = jnp.where(
            low_lanes, total(pl.ds(first_row, half)), total(pl.ds(first_row + half, half))
        )


def cell_sums(ext, node_dev, stiff, connect, scale, live):
    nodes, capacity = connect.shape
    assert capacity % (2 * PAIRS) == 0
    depth = stiff.shape[0]
    rows = ext.shape[0]
    half = (rows - node_dev) // 4
    return pl.pallas_call(
        functools.partial(cell_kernel, nodes, capacity),
        out_shape=[jax.ShapeDtypeStruct((node_dev, LANES), jnp.float32)]
        + [jax.ShapeDtypeStruct((half, LANES), jnp.float32)] * 2,
        in_specs=[SMEM, SMEM, SMEM] + [VMEM] * 2,
        out_specs=[VMEM] * 3,
        scratch_shapes=[pltpu.VMEM((depth, PAIRS * LANES), jnp.float32)] * 4
        + [pltpu.VMEM((rows, LANES), jnp.float32)] * (2 * WAYS),
        compiler_params=pltpu.CompilerParams(vmem_limit_bytes=24 * MIB),
    )(connect, scale, live, stiff, ext.reshape(rows, 1, LANES))


def gather_shared(shared, half, wide, send_low, send_high):
    low_lanes = low_half()
    group = math.gcd(half, 16)

    @pl.loop(0, half // group)
    def _(turn):
        todo = []
        for k in range(group):
            j = turn * group + k
            for side, send in ((0, send_low), (1, send_high)):
                first = wide[pl.ds(shared[side, j], 1), :]
                second = wide[pl.ds(shared[side, j + half], 1), :]
                todo.append((send, pl.ds(j, 1), jnp.where(low_lanes, first, second)))
        for ref, at, value in todo:
            ref[at, :] = value


def gather_kernel(shared, wide, send_low, send_high, packed_low, packed_high):
    half = packed_low.shape[0]
    gather_shared(shared, half, wide, packed_low, packed_high)
    send_low[...] = packed_low[...].astype(send_low.dtype)
    send_high[...] = packed_high[...].astype(send_high.dtype)


def first_sends(shared, wide):
    half = shared.shape[1] // 2
    return pl.pallas_call(
        gather_kernel,
        out_shape=[jax.ShapeDtypeStruct((half, LANES), jnp.bfloat16)] * 2,
        in_specs=[SMEM, VMEM],
        out_specs=[VMEM] * 2,
        scratch_shapes=[pltpu.VMEM((half, LANES), jnp.float32)] * 2,
        compiler_params=pltpu.CompilerParams(vmem_limit_bytes=8 * MIB),
    )(shared, wide)


def assemble_kernel(stage, shared, window, totals, from_low, from_high, potential, before, start, *refs):
    outs = {"first": 3, "second": 6, "third": 1}[stage]
    out, scratch = refs[:outs], refs[outs:]
    sums, scratch = scratch[: 4 * SHARED_WAYS], scratch[4 * SHARED_WAYS :]
    half = from_low.shape[0]
    low_lanes = low_half()
    clear(sums)
    group = math.gcd(half, 8)

    @pl.loop(0, half // group)
    def _(turn):
        for begin in range(0, group, SHARED_WAYS):
            todo = []
            for way in range(SHARED_WAYS):
                j = turn * group + begin + way
                for side, part in ((0, from_low), (1, from_high)):
                    term = part[pl.ds(j, 1), :]
                    for upper in range(2):
                        total = sums[way * 4 + side * 2 + upper]
                        at = pl.ds(shared[side, j + upper * half], 1)
                        todo.append((total, at, total[at, :] + term))
            for ref, at, value in todo:
                ref[at, :] = value

    center = window[0]
    half_width = window[1]
    lows = [sums[k] for k in range(0, len(sums), 2)]
    highs = [sums[k] for k in range(1, len(sums), 2)]

    def pointwise(at):
        both = jnp.where(low_lanes, sum_of(lows, at), sum_of(highs, at))
        value = before[at, :]
        applied = totals[at, :] + (both + swapped(both)) + potential[at, :] * value
        if stage == "first":
            passed = (applied - center * value) * (sigma_one / half_width)
            out[0][at, :] = passed.astype(jnp.bfloat16).astype(jnp.float32)
        elif stage == "second":
            filtered = (applied - center * value) * (
                2.0 * sigma_two / half_width
            ) - sigma_one * sigma_two * start[at, :]
            out[3][at, :] = filtered
            turned = filtered.T[:HALF, :]
            out[4][:, at] = turned
            out[5][:, at] = turned.astype(jnp.bfloat16)
            out[0][at, :] = filtered.astype(jnp.bfloat16).astype(jnp.float32)
        else:
            out[0][at, :] = applied[:, :HALF].astype(jnp.bfloat16)

    chunks(totals.shape[0], pointwise)
    if stage != "third":
        gather_shared(shared, half, out[0], scratch[0], scratch[1])
        out[1][...] = scratch[0][...].astype(out[1].dtype)
        out[2][...] = scratch[1][...].astype(out[2].dtype)


def assemble(stage, shared, window, totals, from_low, from_high, potential, before, start):
    half = from_low.shape[0]
    whole = jax.ShapeDtypeStruct(totals.shape, jnp.float32)
    packed = jax.ShapeDtypeStruct((half, LANES), jnp.bfloat16)
    rows = totals.shape[0]
    out_shape = {
        "first": [whole, packed, packed],
        "second": [
            whole,
            packed,
            packed,
            whole,
            jax.ShapeDtypeStruct((HALF, rows), jnp.float32),
            jax.ShapeDtypeStruct((HALF, rows), jnp.bfloat16),
        ],
        "third": [jax.ShapeDtypeStruct((rows, HALF), jnp.bfloat16)],
    }[stage]
    return pl.pallas_call(
        functools.partial(assemble_kernel, stage),
        out_shape=out_shape,
        in_specs=[SMEM, SMEM] + [VMEM] * 6,
        out_specs=[VMEM] * len(out_shape),
        scratch_shapes=[pltpu.VMEM(totals.shape, jnp.float32)] * (4 * SHARED_WAYS)
        + [pltpu.VMEM((half, LANES), jnp.float32)] * 2,
        compiler_params=pltpu.CompilerParams(vmem_limit_bytes=20 * MIB),
    )(shared, window, totals, from_low, from_high, potential, before, start)


def exchange(count, send_low, send_high, slot_low, slot_high, sems, meanwhile):
    me = lax.axis_index("cells")
    has_low = me > 0
    has_high = me < count - 1
    barrier = pltpu.get_barrier_semaphore()

    @pl.when(has_low)
    def _():
        pl.semaphore_signal(
            barrier, inc=1, device_id={"cells": me - 1}, device_id_type=pl.DeviceIdType.MESH
        )

    @pl.when(has_high)
    def _():
        pl.semaphore_signal(
            barrier, inc=1, device_id={"cells": me + 1}, device_id_type=pl.DeviceIdType.MESH
        )

    pl.semaphore_wait(barrier, jnp.minimum(me, 1) + jnp.minimum(count - 1 - me, 1))

    def copy(source, slot, place, target):
        return pltpu.make_async_remote_copy(
            src_ref=source,
            dst_ref=slot,
            send_sem=sems.at[place],
            recv_sem=sems.at[place + 1],
            device_id={"cells": target},
            device_id_type=pl.DeviceIdType.MESH,
        )

    down = copy(send_low, slot_high, 0, me - 1)
    up = copy(send_high, slot_low, 2, me + 1)

    @pl.when(has_low)
    def _():
        down.start()

    @pl.when(has_high)
    def _():
        up.start()

    meanwhile()

    @pl.when(has_low)
    def _():
        up.wait_recv()

    @pl.when(jnp.logical_not(has_low))
    def _():
        slot_low[...] = jnp.zeros_like(slot_low)

    @pl.when(has_high)
    def _():
        down.wait_recv()

    @pl.when(jnp.logical_not(has_high))
    def _():
        slot_high[...] = jnp.zeros_like(slot_high)

    @pl.when(has_low)
    def _():
        down.wait_send()

    @pl.when(has_high)
    def _():
        up.wait_send()


def extend_kernel(count, own, send_low, send_high, ext, slot_low, slot_high, sems):
    node_dev = own.shape[0]
    half = send_low.shape[0]
    low_lanes = low_half()

    def copy_own(at):
        ext[pl.ds(pl.multiple_of(at.start + 2 * half, at.size), at.size), :] = own[at, :]

    exchange(
        count,
        send_low,
        send_high,
        slot_low,
        slot_high,
        sems,
        lambda: chunks(node_dev, copy_own),
    )
    for first_row, part in ((0, slot_low), (2 * half + node_dev, slot_high)):
        value = part[...].astype(jnp.float32)
        other = swapped(value)
        ext[first_row : first_row + half, :] = jnp.where(low_lanes, value, other)
        ext[first_row + half : first_row + 2 * half, :] = jnp.where(low_lanes, other, value)


def swap_kernel(count, send_low, send_high, from_low, from_high, slot_low, slot_high, sems):
    exchange(count, send_low, send_high, slot_low, slot_high, sems, lambda: None)
    from_low[...] = slot_low[...]
    from_high[...] = slot_high[...]


def exchange_call(kernel, collective_id, out_shape, like, *operands):
    return pl.pallas_call(
        functools.partial(kernel, lax.axis_size("cells")),
        out_shape=out_shape,
        in_specs=[VMEM] * len(operands),
        out_specs=[VMEM] * len(out_shape),
        scratch_shapes=[pltpu.VMEM(like.shape, like.dtype)] * 2
        + [pltpu.SemaphoreType.DMA((4,))],
        compiler_params=pltpu.CompilerParams(
            collective_id=collective_id, has_side_effects=True, vmem_limit_bytes=8 * MIB
        ),
    )(*operands)


def extend(own, send_low, send_high):
    rows = own.shape[0] + 4 * send_low.shape[0]
    shape = jax.ShapeDtypeStruct((rows, LANES), jnp.float32)
    return exchange_call(extend_kernel, 0, [shape], send_low, own, send_low, send_high)[0]


def swap(send_low, send_high):
    shape = jax.ShapeDtypeStruct(send_low.shape, send_low.dtype)
    return exchange_call(swap_kernel, 1, [shape] * 2, send_low, send_low, send_high)


def reduce_kernel(count, parts, out, slots, send_sems, recv_sems):
    me = lax.axis_index("cells")
    barrier = pltpu.get_barrier_semaphore()

    @pl.loop(1, count)
    def _(step):
        pl.semaphore_signal(
            barrier,
            inc=1,
            device_id={"cells": lax.rem(me + step, count)},
            device_id_type=pl.DeviceIdType.MESH,
        )

    pl.semaphore_wait(barrier, count - 1)

    def copy(step):
        target = lax.rem(me + step, count)
        return pltpu.make_async_remote_copy(
            src_ref=parts.at[target],
            dst_ref=slots.at[step],
            send_sem=send_sems.at[step],
            recv_sem=recv_sems.at[step],
            device_id={"cells": target},
            device_id_type=pl.DeviceIdType.MESH,
        )

    @pl.loop(1, count)
    def _(step):
        copy(step).start()

    out[...] = parts[me]

    @pl.loop(1, count)
    def _(step):
        copy(step).wait_recv()
        out[...] += slots[step]

    @pl.loop(1, count)
    def _(step):
        copy(step).wait_send()


def reduce_parts(parts, collective_id):
    count, rows, columns = parts.shape
    return pl.pallas_call(
        functools.partial(reduce_kernel, count),
        out_shape=jax.ShapeDtypeStruct((rows, columns), jnp.float32),
        in_specs=[VMEM],
        out_specs=VMEM,
        scratch_shapes=[
            pltpu.VMEM(parts.shape, jnp.float32),
            pltpu.SemaphoreType.DMA((count,)),
            pltpu.SemaphoreType.DMA((count,)),
        ],
        compiler_params=pltpu.CompilerParams(
            collective_id=collective_id, has_side_effects=True, vmem_limit_bytes=8 * MIB
        ),
    )(parts)


def local(waves, stiffness, cell_scale, potential, connect, live_cells, shared, window):
    columns, node_dev = waves.shape
    assert columns == HALF
    nodes = connect.shape[0]
    depth = -(-nodes // LANES) * LANES
    stiff = jnp.pad(stiffness, ((0, depth - nodes), (0, depth - nodes))).astype(jnp.bfloat16)
    lists = shared[0]
    potential_wide = jnp.broadcast_to(potential[:, None], (node_dev, LANES))
    count = lax.axis_size("cells")

    def totals_of(own, send_low, send_high):
        totals, to_low, to_high = cell_sums(
            extend(own, send_low, send_high), node_dev, stiff, connect, cell_scale, live_cells
        )
        return totals, *swap(to_low, to_high)

    start = jnp.concatenate([waves, waves], axis=0).T.astype(jnp.float32)
    first, *sends = assemble(
        "first",
        lists,
        window,
        *totals_of(start, *first_sends(lists, start)),
        potential_wide,
        start,
        start,
    )
    second, send_low, send_high, filtered, filtered_rows, wave_rows = assemble(
        "second", lists, window, *totals_of(first, *sends), potential_wide, first, start
    )
    gathered = lax.all_gather(wave_rows, "bands", axis=0, tiled=True)
    (apply_rounded,) = assemble(
        "third",
        lists,
        window,
        *totals_of(second, send_low, send_high),
        potential_wide,
        filtered,
        start,
    )
    partial_value = jnp.einsum(
        "wn,nv->wv", gathered, apply_rounded, preferred_element_type=jnp.float32
    ) * (1.0 / (node_dev * count))
    projected = reduce_parts(partial_value.reshape(count, -1, columns), 2)
    return (filtered_rows, projected)


def solution(mesh):
    return jax.shard_map(
        local,
        mesh=mesh,
        in_specs=(
            P("bands", "cells"),
            P(),
            P("cells"),
            P("cells"),
            P(None, "cells"),
            P("cells"),
            P("cells", None, None),
            P(),
        ),
        out_specs=(P("bands", "cells"), P("cells", "bands")),
        check_vma=False,
    )
```

```python
import functools
import math

import jax
import jax.numpy as jnp
from jax import lax
from jax.experimental import pallas as pl
from jax.experimental.pallas import tpu as pltpu
from jax.sharding import PartitionSpec as P

sigma_one = -0.5
sigma_two = 1.0 / (2.0 / sigma_one - sigma_one)

LANES = 128
HALF = LANES // 2
WAYS = 4
TRIP_ROWS = 64
SHARED_WAYS = 2
MIB = 1024 * 1024
VMEM = pl.BlockSpec(memory_space=pltpu.VMEM)
SMEM = pl.BlockSpec(memory_space=pltpu.SMEM)


def low_half():
    return lax.broadcasted_iota(jnp.int32, (1, LANES), 1) < HALF


def swapped(block):
    return pltpu.roll(block, HALF, axis=1)


def chunks(rows, body):
    size = math.gcd(rows, 256)

    @pl.loop(0, rows // size)
    def _(step):
        body(pl.ds(pl.multiple_of(step * size, size), size))


def clear(refs):
    def body(at):
        for ref in refs:
            ref[at, :] = jnp.zeros((at.size, LANES), ref.dtype)

    chunks(refs[0].shape[0], body)


def sum_of(refs, at):
    total = refs[0][at, :]
    for ref in refs[1:]:
        total += ref[at, :]
    return total


def cell_kernel(
    capacity,
    connect,
    scale,
    live,
    stiff,
    ext,
    out,
    out_low,
    out_high,
    x,
    p,
    *sums,
):
    lows, highs = sums[:WAYS], sums[WAYS:]
    node_dev = out.shape[0]
    half = out_low.shape[0]
    low_lanes = low_half()
    clear(sums)

    live_count = live[0]
    pairs = (live_count + 1) // 2
    last = capacity // 2 - 1
    depth = stiff.shape[0]
    x[...] = jnp.zeros_like(x)
    p[...] = jnp.zeros_like(p)

    def first_cell(pair):
        return jnp.clip(pair, 0, last) * 2

    @pl.loop(0, pairs + 2)
    def _(step):
        now = lax.rem(step, 2)
        other = 1 - now
        done = first_cell(step - 2)
        middle = first_cell(step - 1)
        begun = first_cell(step)
        weight = jnp.where(
            low_lanes,
            jnp.where(step * 2 - 2 < live_count, scale[middle], 0.0),
            jnp.where(step * 2 - 1 < live_count, scale[middle + 1], 0.0),
        )

        @pl.loop(0, depth // TRIP_ROWS)
        def _(trip):
            base = pl.multiple_of(trip * TRIP_ROWS, TRIP_ROWS)
            block = pl.ds(base, TRIP_ROWS)
            product = weight * jnp.dot(
                stiff[block, :], x[other].astype(jnp.bfloat16), preferred_element_type=jnp.float32
            )
            for begin in range(0, TRIP_ROWS, WAYS):
                todo = []
                for way in range(WAYS):
                    j = base + begin + way
                    term = p[now, pl.ds(j, 1), :]
                    for total, cell in ((lows[way], done), (highs[way], done + 1)):
                        at = pl.ds(connect[j, cell], 1)
                        todo.append((total, (at, slice(None)), total[at, :] + term))
                    low = ext[connect[j, begun]]
                    high = ext[connect[j, begun + 1]]
                    value = jnp.where(low_lanes, low, high)
                    todo.append((x, (now, pl.ds(j, 1), slice(None)), value))
                for ref, at, value in todo:
                    ref[at] = value
            p[other, block, :] = product

    def total(at):
        both = jnp.where(low_lanes, sum_of(lows, at), sum_of(highs, at))
        return both + swapped(both)

    def write_own(at):
        out[at, :] = total(pl.ds(pl.multiple_of(at.start + 2 * half, at.size), at.size))

    chunks(node_dev, write_own)
    for first_row, part in ((0, out_low), (2 * half + node_dev, out_high)):
        part[...] = jnp.where(
            low_lanes, total(pl.ds(first_row, half)), total(pl.ds(first_row + half, half))
        )


def cell_sums(ext, node_dev, stiff, connect, scale, live):
    capacity = connect.shape[1]
    assert capacity % 2 == 0
    depth = stiff.shape[0]
    rows = ext.shape[0]
    half = (rows - node_dev) // 4
    return pl.pallas_call(
        functools.partial(cell_kernel, capacity),
        out_shape=[jax.ShapeDtypeStruct((node_dev, LANES), jnp.float32)]
        + [jax.ShapeDtypeStruct((half, LANES), jnp.float32)] * 2,
        in_specs=[SMEM, SMEM, SMEM] + [VMEM] * 2,
        out_specs=[VMEM] * 3,
        scratch_shapes=[pltpu.VMEM((2, depth, LANES), jnp.float32)] * 2
        + [pltpu.VMEM((rows, LANES), jnp.float32)] * (2 * WAYS),
        compiler_params=pltpu.CompilerParams(vmem_limit_bytes=24 * MIB),
    )(connect, scale, live, stiff, ext.reshape(rows, 1, LANES))


def gather_shared(shared, half, wide, send_low, send_high):
    low_lanes = low_half()
    group = math.gcd(half, 16)

    @pl.loop(0, half // group)
    def _(turn):
        todo = []
        for k in range(group):
            j = turn * group + k
            for side, send in ((0, send_low), (1, send_high)):
                first = wide[pl.ds(shared[side, j], 1), :]
                second = wide[pl.ds(shared[side, j + half], 1), :]
                todo.append((send, pl.ds(j, 1), jnp.where(low_lanes, first, second)))
        for ref, at, value in todo:
            ref[at, :] = value


def gather_kernel(shared, wide, send_low, send_high, packed_low, packed_high):
    half = packed_low.shape[0]
    gather_shared(shared, half, wide, packed_low, packed_high)
    send_low[...] = packed_low[...].astype(send_low.dtype)
    send_high[...] = packed_high[...].astype(send_high.dtype)


def first_sends(shared, wide):
    half = shared.shape[1] // 2
    return pl.pallas_call(
        gather_kernel,
        out_shape=[jax.ShapeDtypeStruct((half, LANES), jnp.bfloat16)] * 2,
        in_specs=[SMEM, VMEM],
        out_specs=[VMEM] * 2,
        scratch_shapes=[pltpu.VMEM((half, LANES), jnp.float32)] * 2,
        compiler_params=pltpu.CompilerParams(vmem_limit_bytes=8 * MIB),
    )(shared, wide)


def assemble_kernel(stage, shared, window, totals, from_low, from_high, potential, before, start, *refs):
    outs = {"first": 3, "second": 6, "third": 1}[stage]
    out, scratch = refs[:outs], refs[outs:]
    sums, scratch = scratch[: 4 * SHARED_WAYS], scratch[4 * SHARED_WAYS :]
    half = from_low.shape[0]
    low_lanes = low_half()
    clear(sums)
    group = math.gcd(half, 8)

    @pl.loop(0, half // group)
    def _(turn):
        for begin in range(0, group, SHARED_WAYS):
            todo = []
            for way in range(SHARED_WAYS):
                j = turn * group + begin + way
                for side, part in ((0, from_low), (1, from_high)):
                    term = part[pl.ds(j, 1), :]
                    for upper in range(2):
                        total = sums[way * 4 + side * 2 + upper]
                        at = pl.ds(shared[side, j + upper * half], 1)
                        todo.append((total, at, total[at, :] + term))
            for ref, at, value in todo:
                ref[at, :] = value

    center = window[0]
    half_width = window[1]
    lows = [sums[k] for k in range(0, len(sums), 2)]
    highs = [sums[k] for k in range(1, len(sums), 2)]

    def pointwise(at):
        both = jnp.where(low_lanes, sum_of(lows, at), sum_of(highs, at))
        value = before[at, :]
        applied = totals[at, :] + (both + swapped(both)) + potential[at, :] * value
        if stage == "first":
            passed = (applied - center * value) * (sigma_one / half_width)
            out[0][at, :] = passed.astype(jnp.bfloat16).astype(jnp.float32)
        elif stage == "second":
            filtered = (applied - center * value) * (
                2.0 * sigma_two / half_width
            ) - sigma_one * sigma_two * start[at, :]
            out[3][at, :] = filtered
            turned = filtered.T[:HALF, :]
            out[4][:, at] = turned
            out[5][:, at] = turned.astype(jnp.bfloat16)
            out[0][at, :] = filtered.astype(jnp.bfloat16).astype(jnp.float32)
        else:
            out[0][at, :] = applied[:, :HALF].astype(jnp.bfloat16)

    chunks(totals.shape[0], pointwise)
    if stage != "third":
        gather_shared(shared, half, out[0], scratch[0], scratch[1])
        out[1][...] = scratch[0][...].astype(out[1].dtype)
        out[2][...] = scratch[1][...].astype(out[2].dtype)


def assemble(stage, shared, window, totals, from_low, from_high, potential, before, start):
    half = from_low.shape[0]
    whole = jax.ShapeDtypeStruct(totals.shape, jnp.float32)
    packed = jax.ShapeDtypeStruct((half, LANES), jnp.bfloat16)
    rows = totals.shape[0]
    out_shape = {
        "first": [whole, packed, packed],
        "second": [
            whole,
            packed,
            packed,
            whole,
            jax.ShapeDtypeStruct((HALF, rows), jnp.float32),
            jax.ShapeDtypeStruct((HALF, rows), jnp.bfloat16),
        ],
        "third": [jax.ShapeDtypeStruct((rows, HALF), jnp.bfloat16)],
    }[stage]
    return pl.pallas_call(
        functools.partial(assemble_kernel, stage),
        out_shape=out_shape,
        in_specs=[SMEM, SMEM] + [VMEM] * 6,
        out_specs=[VMEM] * len(out_shape),
        scratch_shapes=[pltpu.VMEM(totals.shape, jnp.float32)] * (4 * SHARED_WAYS)
        + [pltpu.VMEM((half, LANES), jnp.float32)] * 2,
        compiler_params=pltpu.CompilerParams(vmem_limit_bytes=20 * MIB),
    )(shared, window, totals, from_low, from_high, potential, before, start)


def exchange(count, send_low, send_high, slot_low, slot_high, sems, meanwhile):
    me = lax.axis_index("cells")
    has_low = me > 0
    has_high = me < count - 1
    barrier = pltpu.get_barrier_semaphore()

    @pl.when(has_low)
    def _():
        pl.semaphore_signal(
            barrier, inc=1, device_id={"cells": me - 1}, device_id_type=pl.DeviceIdType.MESH
        )

    @pl.when(has_high)
    def _():
        pl.semaphore_signal(
            barrier, inc=1, device_id={"cells": me + 1}, device_id_type=pl.DeviceIdType.MESH
        )

    pl.semaphore_wait(barrier, jnp.minimum(me, 1) + jnp.minimum(count - 1 - me, 1))

    def copy(source, slot, place, target):
        return pltpu.make_async_remote_copy(
            src_ref=source,
            dst_ref=slot,
            send_sem=sems.at[place],
            recv_sem=sems.at[place + 1],
            device_id={"cells": target},
            device_id_type=pl.DeviceIdType.MESH,
        )

    down = copy(send_low, slot_high, 0, me - 1)
    up = copy(send_high, slot_low, 2, me + 1)

    @pl.when(has_low)
    def _():
        down.start()

    @pl.when(has_high)
    def _():
        up.start()

    meanwhile()

    @pl.when(has_low)
    def _():
        up.wait_recv()

    @pl.when(jnp.logical_not(has_low))
    def _():
        slot_low[...] = jnp.zeros_like(slot_low)

    @pl.when(has_high)
    def _():
        down.wait_recv()

    @pl.when(jnp.logical_not(has_high))
    def _():
        slot_high[...] = jnp.zeros_like(slot_high)

    @pl.when(has_low)
    def _():
        down.wait_send()

    @pl.when(has_high)
    def _():
        up.wait_send()


def extend_kernel(count, own, send_low, send_high, ext, slot_low, slot_high, sems):
    node_dev = own.shape[0]
    half = send_low.shape[0]
    low_lanes = low_half()

    def copy_own(at):
        ext[pl.ds(pl.multiple_of(at.start + 2 * half, at.size), at.size), :] = own[at, :]

    exchange(
        count,
        send_low,
        send_high,
        slot_low,
        slot_high,
        sems,
        lambda: chunks(node_dev, copy_own),
    )
    for first_row, part in ((0, slot_low), (2 * half + node_dev, slot_high)):
        value = part[...].astype(jnp.float32)
        other = swapped(value)
        ext[first_row : first_row + half, :] = jnp.where(low_lanes, value, other)
        ext[first_row + half : first_row + 2 * half, :] = jnp.where(low_lanes, other, value)


def swap_kernel(count, send_low, send_high, from_low, from_high, slot_low, slot_high, sems):
    exchange(count, send_low, send_high, slot_low, slot_high, sems, lambda: None)
    from_low[...] = slot_low[...]
    from_high[...] = slot_high[...]


def exchange_call(kernel, collective_id, out_shape, like, *operands):
    return pl.pallas_call(
        functools.partial(kernel, lax.axis_size("cells")),
        out_shape=out_shape,
        in_specs=[VMEM] * len(operands),
        out_specs=[VMEM] * len(out_shape),
        scratch_shapes=[pltpu.VMEM(like.shape, like.dtype)] * 2
        + [pltpu.SemaphoreType.DMA((4,))],
        compiler_params=pltpu.CompilerParams(
            collective_id=collective_id, has_side_effects=True, vmem_limit_bytes=8 * MIB
        ),
    )(*operands)


def extend(own, send_low, send_high):
    rows = own.shape[0] + 4 * send_low.shape[0]
    shape = jax.ShapeDtypeStruct((rows, LANES), jnp.float32)
    return exchange_call(extend_kernel, 0, [shape], send_low, own, send_low, send_high)[0]


def swap(send_low, send_high):
    shape = jax.ShapeDtypeStruct(send_low.shape, send_low.dtype)
    return exchange_call(swap_kernel, 1, [shape] * 2, send_low, send_low, send_high)


def reduce_kernel(count, parts, out, slots, send_sems, recv_sems):
    me = lax.axis_index("cells")
    barrier = pltpu.get_barrier_semaphore()

    @pl.loop(1, count)
    def _(step):
        pl.semaphore_signal(
            barrier,
            inc=1,
            device_id={"cells": lax.rem(me + step, count)},
            device_id_type=pl.DeviceIdType.MESH,
        )

    pl.semaphore_wait(barrier, count - 1)

    def copy(step):
        target = lax.rem(me + step, count)
        return pltpu.make_async_remote_copy(
            src_ref=parts.at[target],
            dst_ref=slots.at[step],
            send_sem=send_sems.at[step],
            recv_sem=recv_sems.at[step],
            device_id={"cells": target},
            device_id_type=pl.DeviceIdType.MESH,
        )

    @pl.loop(1, count)
    def _(step):
        copy(step).start()

    out[...] = parts[me]

    @pl.loop(1, count)
    def _(step):
        copy(step).wait_recv()
        out[...] += slots[step]

    @pl.loop(1, count)
    def _(step):
        copy(step).wait_send()


def reduce_parts(parts, collective_id):
    count, rows, columns = parts.shape
    return pl.pallas_call(
        functools.partial(reduce_kernel, count),
        out_shape=jax.ShapeDtypeStruct((rows, columns), jnp.float32),
        in_specs=[VMEM],
        out_specs=VMEM,
        scratch_shapes=[
            pltpu.VMEM(parts.shape, jnp.float32),
            pltpu.SemaphoreType.DMA((count,)),
            pltpu.SemaphoreType.DMA((count,)),
        ],
        compiler_params=pltpu.CompilerParams(
            collective_id=collective_id, has_side_effects=True, vmem_limit_bytes=8 * MIB
        ),
    )(parts)


def local(waves, stiffness, cell_scale, potential, connect, live_cells, shared, window):
    columns, node_dev = waves.shape
    assert columns == HALF
    nodes = connect.shape[0]
    depth = -(-nodes // LANES) * LANES
    stiff = jnp.pad(stiffness, ((0, depth - nodes), (0, depth - nodes))).astype(jnp.bfloat16)
    connect = jnp.pad(connect, ((0, depth - nodes), (0, 0)))
    lists = shared[0]
    potential_wide = jnp.broadcast_to(potential[:, None], (node_dev, LANES))
    count = lax.axis_size("cells")

    def totals_of(own, send_low, send_high):
        totals, to_low, to_high = cell_sums(
            extend(own, send_low, send_high), node_dev, stiff, connect, cell_scale, live_cells
        )
        return totals, *swap(to_low, to_high)

    start = jnp.concatenate([waves, waves], axis=0).T.astype(jnp.float32)
    first, *sends = assemble(
        "first",
        lists,
        window,
        *totals_of(start, *first_sends(lists, start)),
        potential_wide,
        start,
        start,
    )
    second, send_low, send_high, filtered, filtered_rows, wave_rows = assemble(
        "second", lists, window, *totals_of(first, *sends), potential_wide, first, start
    )
    gathered = lax.all_gather(wave_rows, "bands", axis=0, tiled=True)
    (apply_rounded,) = assemble(
        "third",
        lists,
        window,
        *totals_of(second, send_low, send_high),
        potential_wide,
        filtered,
        start,
    )
    partial_value = jnp.einsum(
        "wn,nv->wv", gathered, apply_rounded, preferred_element_type=jnp.float32
    ) * (1.0 / (node_dev * count))
    projected = reduce_parts(partial_value.reshape(count, -1, columns), 2)
    return (filtered_rows, projected)


def solution(mesh):
    return jax.shard_map(
        local,
        mesh=mesh,
        in_specs=(
            P("bands", "cells"),
            P(),
            P("cells"),
            P("cells"),
            P(None, "cells"),
            P("cells"),
            P("cells", None, None),
            P(),
        ),
        out_specs=(P("bands", "cells"), P("cells", "bands")),
        check_vma=False,
    )
```
